32 devices in a mesh: grp: 2 (over y), aux: 2 (over core), ao: 8 (over z, x).
Axes of the slice: x: 2, y: 2, z: 4, core: 2. Of those that a mesh axis runs over, the one named last changes fastest.
Arguments:
- blocks: bfloat16 [16, 2, 64, 64, 32], P(('grp', 'ao'), 'aux'), parts along dimension 0, may hold values from -6 to 6
- occ_density: bfloat16 [16, 64, 64], P(('grp', 'ao')), parts along dimension 0, may hold values from -0.0029296875 to 0.0029296875
- virt_density: bfloat16 [16, 64, 64], P(('grp', 'ao')), parts along dimension 0, may hold values from -0.75 to 0.75
- partner: int32 [16, 2], P(('grp', 'ao'), 'aux'), parts along dimension 0, may hold values from 0 to 7
- screen: int32 [16, 2], P(('grp', 'ao'), 'aux'), parts along dimension 0, may hold values 0 or 1
Outputs:
- chi: float32 [64, 32], P(('grp', 'aux', 'ao')), parts along dimension 0
The draws below stay inside these ranges and needn't reach their ends.
There are 2 independent parts, one for each index of `grp`. The reference program is written for one: setup_inputs(seed, part) draws one part's arguments, and reference() takes and returns one part's arrays. A program takes and returns all parts, laid end to end along the dimension named above; each array names one. Nothing has to cross between parts.
Inputs may be any that keep to these rules, and one draw needn't show every extreme that they name: partner names an atom tile of its own part, an index into that part's 8 tiles.
All inputs are finite; a program needn't handle non-finite values. No bound on the sum of `screen` on one device may be relied on, other than what follows from the above.
Results may differ from the reference program's by a relative error of at most 0.0041.
Values may be sent and summed in bfloat16 or wider, within the bound.
A program may use at most 64 MiB of HBM per device.

```python
import jax
import jax.numpy as jnp
from jax import lax

TILE = 64
NT = 8
SLOTS = 2
NP = 32


def touch_ends(drawn, rng, least, high):
    spot = [jax.random.randint(jax.random.fold_in(rng, axis), (), 0, length) for axis, length in enumerate(drawn.shape)]
    longest = drawn.shape.index(max(drawn.shape))
    neighbour = spot[:longest] + [(spot[longest] + 1) % drawn.shape[longest]] + spot[longest + 1:]
    return drawn.at[tuple(spot)].set(least).at[tuple(neighbour)].set(high)


def block_scale(rng, dims, split, smallest, largest):
    gain = 1.0
    for dim, shards_of in split:
        draws = jax.random.uniform(jax.random.fold_in(jax.random.fold_in(rng, 6), dim), (shards_of,), jnp.float32, smallest / len(split), largest / len(split))
        gain = gain * jnp.repeat(jnp.exp(draws), dims[dim] // shards_of).reshape((-1,) + (1,) * (len(dims) - 1 - dim))
    return gain


def bell_draw(stream_key, shape, width, limit, cuts=(), held_as=jnp.bfloat16):
    loudness = block_scale(stream_key, shape, cuts, -0.22, 0.18) if cuts else 1.0
    result = jax.random.normal(stream_key, shape, jnp.float32) * width * loudness
    return jnp.minimum(jnp.maximum(result, -limit), limit).astype(held_as)


def setup_inputs(seed: int = 0, part: int = 0) -> dict:
    seeds = jax.random.split(jax.random.key(seed), 6)
    part_keys = jax.random.split(jax.random.fold_in(seeds[5], part), 6)
    return {
        "blocks": bell_draw(part_keys[0], (NT, SLOTS, TILE, TILE, NP), 1.0, 6.0, ((0, 8), (1, 2))),
        "occ_density": bell_draw(part_keys[1], (NT, TILE, TILE), (NT * SLOTS * TILE * TILE * TILE) ** -0.5, 0.0029296875, ((0, 8),)),
        "virt_density": bell_draw(part_keys[2], (NT, TILE, TILE), TILE ** -0.5, 0.75, ((0, 8),)),
        "partner": touch_ends(jax.random.randint(part_keys[3], (NT, SLOTS), 0, NT), jax.random.fold_in(part_keys[3], 1), 0, NT - 1).astype(jnp.int32),
        "screen": touch_ends((jax.random.randint(part_keys[4], (NT, SLOTS), 0, 4) < 3).astype(jnp.int32), jax.random.fold_in(part_keys[4], 1), 0, 1),
    }


def reference(blocks, occ_density, virt_density, partner, screen):
    tile_width = blocks.shape[2]
    aux_count = blocks.shape[4]

    def accumulate(running, position):
        row_tile = position // SLOTS
        slot_index = position % SLOTS
        pair_block = blocks[row_tile, slot_index]
        occ_side = jnp.dot(occ_density[row_tile], pair_block.reshape(tile_width, tile_width * aux_count), preferred_element_type=jnp.float32)
        occ_side = occ_side.astype(jnp.bfloat16).reshape(tile_width, tile_width, aux_count)
        virt_block = virt_density[partner[row_tile, slot_index]]
        dressed = jnp.einsum("mnp,nb->mbp", occ_side.astype(jnp.float32), virt_block.astype(jnp.float32))
        dressed = (dressed * screen[row_tile, slot_index].astype(jnp.float32)).astype(jnp.bfloat16)
        dressed = dressed.reshape(tile_width * tile_width, aux_count)
        flat_block = pair_block.reshape(tile_width * tile_width, aux_count)
        chi_term = jnp.dot(dressed.T, flat_block, preferred_element_type=jnp.float32)
        return running + chi_term, None

    start_value = jnp.zeros((aux_count, aux_count), jnp.float32)
    positions = jnp.arange(NT * SLOTS, dtype=jnp.int32)
    running, unused = lax.scan(accumulate, start_value, positions)
    return running
```

```python
import functools

import jax
import jax.numpy as jnp
from jax import lax
from jax.experimental import pallas as pl
from jax.experimental.pallas import tpu as pltpu
from jax.sharding import PartitionSpec as P

MESH = pl.DeviceIdType.MESH
GROUP = 8
KERNEL_ELEMENTS = 1 << 18


def chi_kernel(aux_size, ao_size, blocks_hbm, occ_hbm, virt_hbm, partner_hbm, screen_hbm, chi_out,
               pair, occ, virts, target, survives, outgoing, incoming,
               load_sem, virt_send, virt_recv, chi_send, chi_recv):
    width, aux_count = pair.shape[0], pair.shape[1]
    devices = aux_size * ao_size
    rows = aux_count // devices
    my_aux, my_ao = lax.axis_index("aux"), lax.axis_index("ao")
    me = my_aux * ao_size + my_ao

    loads = [
        pltpu.make_async_copy(blocks_hbm, pair, load_sem.at[0]),
        pltpu.make_async_copy(occ_hbm.at[0], occ, load_sem.at[1]),
        pltpu.make_async_copy(partner_hbm, target, load_sem.at[2]),
        pltpu.make_async_copy(screen_hbm, survives, load_sem.at[3]),
    ]
    for load in loads:
        load.start()
    own_virt = pltpu.make_async_copy(virt_hbm.at[0], virts.at[my_ao], load_sem.at[4])
    own_virt.start()

    def peer(step):
        other = lax.rem(me + step, devices)
        return other, {"aux": lax.div(other, ao_size), "ao": lax.rem(other, ao_size)}

    barrier = pltpu.get_barrier_semaphore()
    for step in range(1, devices):
        pl.semaphore_signal(barrier, inc=1, device_id=peer(step)[1], device_id_type=MESH)
    pl.semaphore_wait(barrier, devices - 1)

    virt_copies = []
    for step in range(1, ao_size):
        copy = pltpu.make_async_remote_copy(
            src_ref=virt_hbm.at[0], dst_ref=virts.at[my_ao],
            send_sem=virt_send.at[step - 1], recv_sem=virt_recv.at[step - 1],
            device_id={"ao": lax.rem(my_ao + step, ao_size)}, device_id_type=MESH)
        copy.start()
        virt_copies.append(copy)

    for load in loads:
        load.wait()
    stack = pair[...]
    by_aux = jnp.swapaxes(stack.astype(jnp.float32), 0, 1).astype(jnp.bfloat16)
    occ_block = occ[...]
    left = jnp.stack([
        jnp.dot(occ_block, by_aux[index], preferred_element_type=jnp.float32)
        for index in range(aux_count)
    ])
    left = jnp.swapaxes(left, 0, 1).astype(jnp.bfloat16).reshape(width * aux_count, width)

    own_virt.wait()
    for copy in virt_copies:
        copy.wait()
    chosen = virts[target[0, 0]]
    flat = stack.reshape(width * aux_count, width)
    right = lax.dot_general(flat, chosen, (((1,), (1,)), ((), ())), preferred_element_type=jnp.float32)
    right = right.astype(jnp.bfloat16)

    span = GROUP * aux_count
    gram = jnp.zeros((span, span), jnp.float32)
    for start in range(0, width * aux_count, span):
        gram += lax.dot_general(left[start:start + span], right[start:start + span],
                                (((1,), (1,)), ((), ())), preferred_element_type=jnp.float32)
    lane = lax.broadcasted_iota(jnp.int32, (aux_count, span), 1)
    wide = jnp.zeros((aux_count, span), jnp.float32)
    for index in range(GROUP):
        low = index * aux_count
        wide = jnp.where((lane >= low) & (lane < low + aux_count), gram[low:low + aux_count], wide)
    chi = wide[:, :aux_count]
    for index in range(1, GROUP):
        chi += wide[:, index * aux_count:(index + 1) * aux_count]
    chi = chi * survives[0, 0].astype(jnp.float32)

    for index in range(devices):
        outgoing[index] = chi[index * rows:(index + 1) * rows]
    chi_copies = []
    for step in range(1, devices):
        other, device = peer(step)
        copy = pltpu.make_async_remote_copy(
            src_ref=outgoing.at[other], dst_ref=incoming.at[me],
            send_sem=chi_send.at[step - 1], recv_sem=chi_recv.at[step - 1],
            device_id=device, device_id_type=MESH)
        copy.start()
        chi_copies.append(copy)
    incoming[me] = outgoing[me]
    for copy in chi_copies:
        copy.wait()
    chi_out[...] = jnp.sum(incoming[...], axis=0)


def fused_shards(aux_size, ao_size, blocks, occ_density, virt_density, partner, screen):
    width, aux_count = blocks.shape[2], blocks.shape[4]
    devices = aux_size * ao_size
    rows = aux_count // devices
    pair = jnp.swapaxes(blocks[0, 0], 1, 2)
    hbm = pl.BlockSpec(memory_space=pl.ANY)
    return pl.pallas_call(
        functools.partial(chi_kernel, aux_size, ao_size),
        out_shape=jax.ShapeDtypeStruct((rows, aux_count), jnp.float32),
        in_specs=[hbm] * 5,
        out_specs=pl.BlockSpec(memory_space=pltpu.VMEM),
        scratch_shapes=[
            pltpu.VMEM((width, aux_count, width), jnp.bfloat16),
            pltpu.VMEM((width, width), jnp.bfloat16),
            pltpu.VMEM((ao_size, width, width), jnp.bfloat16),
            pltpu.SMEM((1, 1), jnp.int32),
            pltpu.SMEM((1, 1), jnp.int32),
            pltpu.VMEM((devices, rows, aux_count), jnp.float32),
            pltpu.VMEM((devices, rows, aux_count), jnp.float32),
            pltpu.SemaphoreType.DMA((5,)),
            pltpu.SemaphoreType.DMA((ao_size - 1,)),
            pltpu.SemaphoreType.DMA((ao_size - 1,)),
            pltpu.SemaphoreType.DMA((devices - 1,)),
            pltpu.SemaphoreType.DMA((devices - 1,)),
        ],
        compiler_params=pltpu.CompilerParams(
            collective_id=0, has_side_effects=True, vmem_limit_bytes=32 << 20
        ),
    )(pair, occ_density, virt_density, partner, screen)


def staged_shards(blocks, occ_density, virt_density, partner, screen):
    tile_width = blocks.shape[2]
    aux_count = blocks.shape[4]
    target = partner[0, 0]
    gathered = lax.all_gather(virt_density, "ao", axis=0, tiled=True)
    chosen = lax.dynamic_index_in_dim(gathered, target, 0, keepdims=False)
    pair_block = blocks[0, 0]
    occ_side = jnp.dot(
        occ_density[0],
        pair_block.reshape(tile_width, tile_width * aux_count),
        preferred_element_type=jnp.float32,
    )
    occ_side = occ_side.astype(jnp.bfloat16).reshape(tile_width, tile_width, aux_count)
    dressed = jnp.einsum("mnp,nb->mbp", occ_side, chosen, preferred_element_type=jnp.float32)
    dressed = (dressed * screen[0, 0].astype(jnp.float32)).astype(jnp.bfloat16)
    dressed = dressed.reshape(tile_width * tile_width, aux_count)
    flat_block = pair_block.reshape(tile_width * tile_width, aux_count)
    chi_term = lax.dot_general(
        dressed, flat_block, (((0,), (0,)), ((), ())), preferred_element_type=jnp.float32
    )
    half_sum = lax.psum_scatter(chi_term, "aux", scatter_dimension=0, tiled=True)
    return lax.psum_scatter(half_sum, "ao", scatter_dimension=0, tiled=True)


def solution(mesh):
    aux_size, ao_size = mesh.shape["aux"], mesh.shape["ao"]
    placed = (
        P(("grp", "ao"), "aux", None, None, None),
        P(("grp", "ao"), None, None),
        P(("grp", "ao"), None, None),
        P(("grp", "ao"), "aux"),
        P(("grp", "ao"), "aux"),
    )

    def shards(blocks, *rest):
        if blocks.size <= KERNEL_ELEMENTS:
            return fused_shards(aux_size, ao_size, blocks, *rest)
        return staged_shards(blocks, *rest)

    return jax.shard_map(
        shards, mesh=mesh, in_specs=placed, out_specs=P(("grp", "aux", "ao"), None), check_vma=False
    )
```

```python
import functools

import jax
import jax.numpy as jnp
from jax import lax
from jax.experimental import pallas as pl
from jax.experimental.pallas import tpu as pltpu
from jax.sharding import PartitionSpec as P

MESH = pl.DeviceIdType.MESH
GROUP = 8
KERNEL_ELEMENTS = 1 << 18


def flipped(position, mask, count):
    other, bit = position, 1
    while bit < count:
        if mask & bit:
            other = other + (1 - 2 * lax.rem(lax.div(position, bit), 2)) * bit
        bit *= 2
    return other


def chi_kernel(aux_size, ao_size, blocks_hbm, occ_hbm, virt_hbm, partner_hbm, screen_hbm, chi_out,
               pair, occ, own_virt, virts, target, survives, outgoing, incoming,
               load_sem, virt_send, virt_recv, chi_send, chi_recv):
    width, aux_count = pair.shape[0], pair.shape[1]
    devices = aux_size * ao_size
    rows = aux_count // devices
    my_aux, my_ao = lax.axis_index("aux"), lax.axis_index("ao")
    me = my_aux * ao_size + my_ao

    peers = []
    for ao_mask in range(ao_size - 1, -1, -1):
        for aux_mask in range(aux_size - 1, -1, -1):
            if ao_mask or aux_mask:
                aux, ao = flipped(my_aux, aux_mask, aux_size), flipped(my_ao, ao_mask, ao_size)
                peers.append((aux * ao_size + ao, {"aux": aux, "ao": ao}))

    barrier = pltpu.get_barrier_semaphore()
    for _, device in peers:
        pl.semaphore_signal(barrier, inc=1, device_id=device, device_id_type=MESH)

    virt_load = pltpu.make_async_copy(virt_hbm.at[0], own_virt, load_sem.at[4])
    virt_load.start()
    loads = [
        pltpu.make_async_copy(blocks_hbm, pair, load_sem.at[0]),
        pltpu.make_async_copy(occ_hbm.at[0], occ, load_sem.at[1]),
        pltpu.make_async_copy(partner_hbm, target, load_sem.at[2]),
        pltpu.make_async_copy(screen_hbm, survives, load_sem.at[3]),
    ]
    for load in loads:
        load.start()
    half = width // 2
    virt_load.wait()
    virts[my_ao] = jnp.concatenate([own_virt[:half], own_virt[half:]], axis=1)

    pl.semaphore_wait(barrier, devices - 1)
    virt_copies = []
    for ao_mask in range(ao_size - 1, 0, -1):
        copy = pltpu.make_async_remote_copy(
            src_ref=virts.at[my_ao], dst_ref=virts.at[my_ao],
            send_sem=virt_send.at[ao_mask - 1], recv_sem=virt_recv.at[ao_mask - 1],
            device_id={"ao": flipped(my_ao, ao_mask, ao_size)}, device_id_type=MESH)
        copy.start()
        virt_copies.append(copy)

    for load in loads:
        load.wait()
    stack = pair[...]
    by_aux = jnp.swapaxes(stack.astype(jnp.float32), 0, 1).astype(jnp.bfloat16)
    occ_block = occ[...]
    left = jnp.stack([
        jnp.dot(occ_block, by_aux[index], preferred_element_type=jnp.float32)
        for index in range(aux_count)
    ])
    left = jnp.swapaxes(left, 0, 1).astype(jnp.bfloat16).reshape(width * aux_count, width)

    for copy in reversed(virt_copies):
        copy.wait_recv()
    chosen = virts[target[0, 0]]
    chosen = jnp.concatenate([chosen[:, :width], chosen[:, width:]], axis=0)
    flat = stack.reshape(width * aux_count, width)
    right = lax.dot_general(flat, chosen, (((1,), (1,)), ((), ())), preferred_element_type=jnp.float32)
    right = right.astype(jnp.bfloat16)

    span = GROUP * aux_count
    gram = jnp.zeros((span, span), jnp.float32)
    for start in range(0, width * aux_count, span):
        gram += lax.dot_general(left[start:start + span], right[start:start + span],
                                (((1,), (1,)), ((), ())), preferred_element_type=jnp.float32)
    lane = lax.broadcasted_iota(jnp.int32, (aux_count, span), 1)
    wide = jnp.zeros((aux_count, span), jnp.float32)
    for index in range(GROUP):
        low = index * aux_count
        wide = jnp.where((lane >= low) & (lane < low + aux_count), gram[low:low + aux_count], wide)
    chi = wide[:, :aux_count]
    for index in range(1, GROUP):
        chi += wide[:, index * aux_count:(index + 1) * aux_count]
    chi = chi * survives[0, 0].astype(jnp.float32)

    for index in range(devices):
        outgoing[index] = chi[index * rows:(index + 1) * rows]
    chi_copies = []
    for index, (other, device) in enumerate(peers):
        copy = pltpu.make_async_remote_copy(
            src_ref=outgoing.at[other], dst_ref=incoming.at[me],
            send_sem=chi_send.at[index], recv_sem=chi_recv.at[index],
            device_id=device, device_id_type=MESH)
        copy.start()
        chi_copies.append(copy)
    incoming[me] = outgoing[me]
    for copy in virt_copies + chi_copies:
        copy.wait_send()
    for copy in reversed(chi_copies):
        copy.wait_recv()
    chi_out[...] = jnp.sum(incoming[...], axis=0)


def fused_shards(aux_size, ao_size, blocks, occ_density, virt_density, partner, screen):
    width, aux_count = blocks.shape[2], blocks.shape[4]
    devices = aux_size * ao_size
    rows = aux_count // devices
    pair = jnp.swapaxes(blocks[0, 0], 1, 2)
    hbm = pl.BlockSpec(memory_space=pl.ANY)
    return pl.pallas_call(
        functools.partial(chi_kernel, aux_size, ao_size),
        out_shape=jax.ShapeDtypeStruct((rows, aux_count), jnp.float32),
        in_specs=[hbm] * 5,
        out_specs=pl.BlockSpec(memory_space=pltpu.VMEM),
        scratch_shapes=[
            pltpu.VMEM((width, aux_count, width), jnp.bfloat16),
            pltpu.VMEM((width, width), jnp.bfloat16),
            pltpu.VMEM((width, width), jnp.bfloat16),
            pltpu.VMEM((ao_size, width // 2, 2 * width), jnp.bfloat16),
            pltpu.SMEM((1, 1), jnp.int32),
            pltpu.SMEM((1, 1), jnp.int32),
            pltpu.VMEM((devices, rows, aux_count), jnp.float32),
            pltpu.VMEM((devices, rows, aux_count), jnp.float32),
            pltpu.SemaphoreType.DMA((5,)),
            pltpu.SemaphoreType.DMA((ao_size - 1,)),
            pltpu.SemaphoreType.DMA((ao_size - 1,)),
            pltpu.SemaphoreType.DMA((devices - 1,)),
            pltpu.SemaphoreType.DMA((devices - 1,)),
        ],
        compiler_params=pltpu.CompilerParams(
            collective_id=0, has_side_effects=True, vmem_limit_bytes=60 << 20
        ),
    )(pair, occ_density, virt_density, partner, screen)


def staged_shards(blocks, occ_density, virt_density, partner, screen):
    tile_width = blocks.shape[2]
    aux_count = blocks.shape[4]
    target = partner[0, 0]
    gathered = lax.all_gather(virt_density, "ao", axis=0, tiled=True)
    chosen = lax.dynamic_index_in_dim(gathered, target, 0, keepdims=False)
    pair_block = blocks[0, 0]
    occ_side = jnp.dot(
        occ_density[0],
        pair_block.reshape(tile_width, tile_width * aux_count),
        preferred_element_type=jnp.float32,
    )
    occ_side = occ_side.astype(jnp.bfloat16).reshape(tile_width, tile_width, aux_count)
    dressed = jnp.einsum("mnp,nb->mbp", occ_side, chosen, preferred_element_type=jnp.float32)
    dressed = (dressed * screen[0, 0].astype(jnp.float32)).astype(jnp.bfloat16)
    dressed = dressed.reshape(tile_width * tile_width, aux_count)
    flat_block = pair_block.reshape(tile_width * tile_width, aux_count)
    chi_term = lax.dot_general(
        dressed, flat_block, (((0,), (0,)), ((), ())), preferred_element_type=jnp.float32
    )
    half_sum = lax.psum_scatter(chi_term, "aux", scatter_dimension=0, tiled=True)
    return lax.psum_scatter(half_sum, "ao", scatter_dimension=0, tiled=True)


def solution(mesh):
    aux_size, ao_size = mesh.shape["aux"], mesh.shape["ao"]
    placed = (
        P(("grp", "ao"), "aux", None, None, None),
        P(("grp", "ao"), None, None),
        P(("grp", "ao"), None, None),
        P(("grp", "ao"), "aux"),
        P(("grp", "ao"), "aux"),
    )

    devices = aux_size * ao_size

    def shards(blocks, *rest):
        if blocks.size <= KERNEL_ELEMENTS and devices & (devices - 1) == 0:
            return fused_shards(aux_size, ao_size, blocks, *rest)
        return staged_shards(blocks, *rest)

    return jax.shard_map(
        shards, mesh=mesh, in_specs=placed, out_specs=P(("grp", "aux", "ao"), None), check_vma=False
    )
```

```python
import functools

import jax
import jax.numpy as jnp
from jax import lax
from jax.experimental import pallas as pl
from jax.experimental.pallas import tpu as pltpu
from jax.sharding import PartitionSpec as P

MESH = pl.DeviceIdType.MESH
GROUP = 8
KERNEL_ELEMENTS = 1 << 18


def flipped(position, mask, count):
    other, bit = position, 1
    while bit < count:
        if mask & bit:
            other = other + (1 - 2 * lax.rem(lax.div(position, bit), 2)) * bit
        bit *= 2
    return other


def chi_kernel(aux_size, ao_size, blocks_hbm, occ_hbm, virt_hbm, partner_hbm, screen_hbm, incoming,
               pair, occ, own_virt, virts, target, survives, outgoing,
               load_sem, virt_send, virt_recv, chi_send, chi_recv):
    width, aux_count = pair.shape[0], pair.shape[1]
    devices = aux_size * ao_size
    rows = aux_count // devices
    my_aux, my_ao = lax.axis_index("aux"), lax.axis_index("ao")
    me = my_aux * ao_size + my_ao

    peers = []
    for ao_mask in range(ao_size - 1, -1, -1):
        for aux_mask in range(aux_size - 1, -1, -1):
            if ao_mask or aux_mask:
                aux, ao = flipped(my_aux, aux_mask, aux_size), flipped(my_ao, ao_mask, ao_size)
                peers.append((aux * ao_size + ao, {"aux": aux, "ao": ao}))

    barrier = pltpu.get_barrier_semaphore()
    for _, device in peers:
        pl.semaphore_signal(barrier, inc=1, device_id=device, device_id_type=MESH)

    virt_load = pltpu.make_async_copy(virt_hbm.at[0], own_virt, load_sem.at[4])
    virt_load.start()
    loads = [
        pltpu.make_async_copy(blocks_hbm, pair, load_sem.at[0]),
        pltpu.make_async_copy(occ_hbm.at[0], occ, load_sem.at[1]),
        pltpu.make_async_copy(partner_hbm, target, load_sem.at[2]),
        pltpu.make_async_copy(screen_hbm, survives, load_sem.at[3]),
    ]
    for load in loads:
        load.start()
    half = width // 2
    virt_load.wait()
    virts[my_ao] = jnp.concatenate([own_virt[:half], own_virt[half:]], axis=1)

    pl.semaphore_wait(barrier, devices - 1)
    virt_copies = []
    for ao_mask in range(ao_size - 1, 0, -1):
        copy = pltpu.make_async_remote_copy(
            src_ref=virts.at[my_ao], dst_ref=virts.at[my_ao],
            send_sem=virt_send.at[ao_mask - 1], recv_sem=virt_recv.at[ao_mask - 1],
            device_id={"ao": flipped(my_ao, ao_mask, ao_size)}, device_id_type=MESH)
        copy.start()
        virt_copies.append(copy)

    for load in loads:
        load.wait()
    stack = pair[...]
    by_aux = jnp.swapaxes(stack.astype(jnp.float32), 0, 1).astype(jnp.bfloat16)
    occ_block = occ[...]
    left = jnp.stack([
        jnp.dot(occ_block, by_aux[index], preferred_element_type=jnp.float32)
        for index in range(aux_count)
    ])
    left = jnp.swapaxes(left, 0, 1).astype(jnp.bfloat16).reshape(width * aux_count, width)

    for copy in reversed(virt_copies):
        copy.wait_recv()
    chosen = virts[target[0, 0]]
    chosen = jnp.concatenate([chosen[:, :width], chosen[:, width:]], axis=0)
    flat = stack.reshape(width * aux_count, width)
    right = lax.dot_general(flat, chosen, (((1,), (1,)), ((), ())), preferred_element_type=jnp.float32)
    right = right.astype(jnp.bfloat16)

    span = GROUP * aux_count
    gram = jnp.zeros((span, span), jnp.float32)
    for start in range(0, width * aux_count, span):
        gram += lax.dot_general(left[start:start + span], right[start:start + span],
                                (((1,), (1,)), ((), ())), preferred_element_type=jnp.float32)
    lane = lax.broadcasted_iota(jnp.int32, (aux_count, span), 1)
    wide = jnp.zeros((aux_count, span), jnp.float32)
    for index in range(GROUP):
        low = index * aux_count
        wide = jnp.where((lane >= low) & (lane < low + aux_count), gram[low:low + aux_count], wide)
    chi = wide[:, :aux_count]
    for index in range(1, GROUP):
        chi += wide[:, index * aux_count:(index + 1) * aux_count]
    chi = chi * survives[0, 0].astype(jnp.float32)

    for index in range(devices):
        outgoing[index] = chi[index * rows:(index + 1) * rows]
    chi_copies = []
    for index, (other, device) in enumerate(peers):
        copy = pltpu.make_async_remote_copy(
            src_ref=outgoing.at[other], dst_ref=incoming.at[me],
            send_sem=chi_send.at[index], recv_sem=chi_recv.at[index],
            device_id=device, device_id_type=MESH)
        copy.start()
        chi_copies.append(copy)
    incoming[me] = outgoing[me]
    for copy in virt_copies + chi_copies:
        copy.wait_send()
    for copy in reversed(chi_copies):
        copy.wait_recv()


def fused_shards(aux_size, ao_size, blocks, occ_density, virt_density, partner, screen):
    width, aux_count = blocks.shape[2], blocks.shape[4]
    devices = aux_size * ao_size
    rows = aux_count // devices
    pair = jnp.swapaxes(blocks[0, 0], 1, 2)
    hbm = pl.BlockSpec(memory_space=pl.ANY)
    terms = pl.pallas_call(
        functools.partial(chi_kernel, aux_size, ao_size),
        out_shape=pltpu.VMEM((devices, rows, aux_count), jnp.float32),
        in_specs=[hbm] * 5,
        out_specs=pl.BlockSpec(memory_space=pltpu.VMEM),
        scratch_shapes=[
            pltpu.VMEM((width, aux_count, width), jnp.bfloat16),
            pltpu.VMEM((width, width), jnp.bfloat16),
            pltpu.VMEM((width, width), jnp.bfloat16),
            pltpu.VMEM((ao_size, width // 2, 2 * width), jnp.bfloat16),
            pltpu.SMEM((1, 1), jnp.int32),
            pltpu.SMEM((1, 1), jnp.int32),
            pltpu.VMEM((devices, rows, aux_count), jnp.float32),
            pltpu.SemaphoreType.DMA((5,)),
            pltpu.SemaphoreType.DMA((ao_size - 1,)),
            pltpu.SemaphoreType.DMA((ao_size - 1,)),
            pltpu.SemaphoreType.DMA((devices - 1,)),
            pltpu.SemaphoreType.DMA((devices - 1,)),
        ],
        compiler_params=pltpu.CompilerParams(
            collective_id=0, has_side_effects=True, vmem_limit_bytes=60 << 20
        ),
    )(pair, occ_density, virt_density, partner, screen)
    return jnp.sum(terms, axis=0)


def staged_shards(blocks, occ_density, virt_density, partner, screen):
    tile_width = blocks.shape[2]
    aux_count = blocks.shape[4]
    target = partner[0, 0]
    gathered = lax.all_gather(virt_density, "ao", axis=0, tiled=True)
    chosen = lax.dynamic_index_in_dim(gathered, target, 0, keepdims=False)
    pair_block = blocks[0, 0]
    occ_side = jnp.dot(
        occ_density[0],
        pair_block.reshape(tile_width, tile_width * aux_count),
        preferred_element_type=jnp.float32,
    )
    occ_side = occ_side.astype(jnp.bfloat16).reshape(tile_width, tile_width, aux_count)
    dressed = jnp.einsum("mnp,nb->mbp", occ_side, chosen, preferred_element_type=jnp.float32)
    dressed = (dressed * screen[0, 0].astype(jnp.float32)).astype(jnp.bfloat16)
    dressed = dressed.reshape(tile_width * tile_width, aux_count)
    flat_block = pair_block.reshape(tile_width * tile_width, aux_count)
    chi_term = lax.dot_general(
        dressed, flat_block, (((0,), (0,)), ((), ())), preferred_element_type=jnp.float32
    )
    half_sum = lax.psum_scatter(chi_term, "aux", scatter_dimension=0, tiled=True)
    return lax.psum_scatter(half_sum, "ao", scatter_dimension=0, tiled=True)


def solution(mesh):
    aux_size, ao_size = mesh.shape["aux"], mesh.shape["ao"]
    placed = (
        P(("grp", "ao"), "aux", None, None, None),
        P(("grp", "ao"), None, None),
        P(("grp", "ao"), None, None),
        P(("grp", "ao"), "aux"),
        P(("grp", "ao"), "aux"),
    )

    devices = aux_size * ao_size

    def shards(blocks, *rest):
        if blocks.size <= KERNEL_ELEMENTS and devices & (devices - 1) == 0:
            return fused_shards(aux_size, ao_size, blocks, *rest)
        return staged_shards(blocks, *rest)

    return jax.shard_map(
        shards, mesh=mesh, in_specs=placed, out_specs=P(("grp", "aux", "ao"), None), check_vma=False
    )
```

```python
import functools

import jax
import jax.numpy as jnp
from jax import lax
from jax.experimental import pallas as pl
from jax.experimental.pallas import tpu as pltpu
from jax.sharding import PartitionSpec as P

MESH = pl.DeviceIdType.MESH
GROUP = 8
PACK = 4
KERNEL_ELEMENTS = 1 << 18


def flipped(position, mask, count):
    other, bit = position, 1
    while bit < count:
        if mask & bit:
            other = other + (1 - 2 * lax.rem(lax.div(position, bit), 2)) * bit
        bit *= 2
    return other


def packed(rows):
    run = rows.shape[0] // PACK
    return jnp.concatenate([rows[index * run:(index + 1) * run] for index in range(PACK)], axis=1)


def chi_kernel(aux_size, ao_size, blocks_hbm, occ_hbm, virt_hbm, partner_hbm, screen_hbm, incoming,
               pair, occ, own_virt, virts, target, survives, outgoing,
               load_sem, virt_send, virt_recv, chi_send, chi_recv):
    width, aux_count = pair.shape[0], pair.shape[1]
    devices = aux_size * ao_size
    rows = aux_count // devices
    my_aux, my_ao = lax.axis_index("aux"), lax.axis_index("ao")
    me = my_aux * ao_size + my_ao

    peers = []
    for ao_mask in range(ao_size - 1, -1, -1):
        for aux_mask in range(aux_size - 1, -1, -1):
            if ao_mask or aux_mask:
                aux, ao = flipped(my_aux, aux_mask, aux_size), flipped(my_ao, ao_mask, ao_size)
                peers.append((aux * ao_size + ao, {"aux": aux, "ao": ao}))

    barrier = pltpu.get_barrier_semaphore()
    for _, device in peers:
        pl.semaphore_signal(barrier, inc=1, device_id=device, device_id_type=MESH)

    virt_load = pltpu.make_async_copy(virt_hbm.at[0], own_virt, load_sem.at[4])
    virt_load.start()
    loads = [
        pltpu.make_async_copy(blocks_hbm, pair, load_sem.at[0]),
        pltpu.make_async_copy(occ_hbm.at[0], occ, load_sem.at[1]),
        pltpu.make_async_copy(partner_hbm, target, load_sem.at[2]),
        pltpu.make_async_copy(screen_hbm, survives, load_sem.at[3]),
    ]
    for load in loads:
        load.start()
    half = width // 2
    virt_load.wait()
    virts[my_ao] = jnp.concatenate([own_virt[:half], own_virt[half:]], axis=1)

    pl.semaphore_wait(barrier, devices - 1)
    virt_copies = []
    for ao_mask in range(ao_size - 1, 0, -1):
        copy = pltpu.make_async_remote_copy(
            src_ref=virts.at[my_ao], dst_ref=virts.at[my_ao],
            send_sem=virt_send.at[ao_mask - 1], recv_sem=virt_recv.at[ao_mask - 1],
            device_id={"ao": flipped(my_ao, ao_mask, ao_size)}, device_id_type=MESH)
        copy.start()
        virt_copies.append(copy)

    for load in loads:
        load.wait()
    stack = pair[...]
    by_aux = jnp.swapaxes(stack.astype(jnp.float32), 0, 1).astype(jnp.bfloat16)
    occ_block = occ[...]
    left = jnp.stack([
        jnp.dot(occ_block, by_aux[index], preferred_element_type=jnp.float32)
        for index in range(aux_count)
    ])
    left = packed(jnp.swapaxes(left, 0, 1).astype(jnp.bfloat16).reshape(width * aux_count, width))
    flat = packed(stack.reshape(width * aux_count, width))

    for copy in reversed(virt_copies):
        copy.wait_recv()
    chosen = virts[target[0, 0]]
    chosen = jnp.concatenate([chosen[:, :width], chosen[:, width:]], axis=0)
    chosen = jnp.concatenate([chosen] * PACK, axis=1)
    side = lax.div(lax.broadcasted_iota(jnp.int32, chosen.shape, 1), width)
    blank = jnp.zeros_like(chosen)
    diagonal = jnp.concatenate([jnp.where(side == index, chosen, blank) for index in range(PACK)], axis=0)
    right = lax.dot_general(flat, diagonal, (((1,), (1,)), ((), ())), preferred_element_type=jnp.float32)
    right = right.astype(jnp.bfloat16)

    span = GROUP * aux_count
    gram = jnp.zeros((span, span), jnp.float32)
    for start in range(0, flat.shape[0], span):
        gram += lax.dot_general(left[start:start + span], right[start:start + span],
                                (((1,), (1,)), ((), ())), preferred_element_type=jnp.float32)
    lane = lax.broadcasted_iota(jnp.int32, (aux_count, span), 1)
    wide = jnp.zeros((aux_count, span), jnp.float32)
    for index in range(GROUP):
        low = index * aux_count
        wide = jnp.where((lane >= low) & (lane < low + aux_count), gram[low:low + aux_count], wide)
    chi = wide[:, :aux_count]
    for index in range(1, GROUP):
        chi += wide[:, index * aux_count:(index + 1) * aux_count]
    chi = chi * survives[0, 0].astype(jnp.float32)

    for index in range(devices):
        outgoing[index] = chi[index * rows:(index + 1) * rows]
    chi_copies = []
    for index, (other, device) in enumerate(peers):
        copy = pltpu.make_async_remote_copy(
            src_ref=outgoing.at[other], dst_ref=incoming.at[me],
            send_sem=chi_send.at[index], recv_sem=chi_recv.at[index],
            device_id=device, device_id_type=MESH)
        copy.start()
        chi_copies.append(copy)
    incoming[me] = outgoing[me]
    for copy in virt_copies + chi_copies:
        copy.wait_send()
    for copy in reversed(chi_copies):
        copy.wait_recv()


def fused_shards(aux_size, ao_size, blocks, occ_density, virt_density, partner, screen):
    width, aux_count = blocks.shape[2], blocks.shape[4]
    devices = aux_size * ao_size
    rows = aux_count // devices
    pair = jnp.swapaxes(blocks[0, 0], 1, 2)
    hbm = pl.BlockSpec(memory_space=pl.ANY)
    terms = pl.pallas_call(
        functools.partial(chi_kernel, aux_size, ao_size),
        out_shape=pltpu.VMEM((devices, rows, aux_count), jnp.float32),
        in_specs=[hbm] * 5,
        out_specs=pl.BlockSpec(memory_space=pltpu.VMEM),
        scratch_shapes=[
            pltpu.VMEM((width, aux_count, width), jnp.bfloat16),
            pltpu.VMEM((width, width), jnp.bfloat16),
            pltpu.VMEM((width, width), jnp.bfloat16),
            pltpu.VMEM((ao_size, width // 2, 2 * width), jnp.bfloat16),
            pltpu.SMEM((1, 1), jnp.int32),
            pltpu.SMEM((1, 1), jnp.int32),
            pltpu.VMEM((devices, rows, aux_count), jnp.float32),
            pltpu.SemaphoreType.DMA((5,)),
            pltpu.SemaphoreType.DMA((ao_size - 1,)),
            pltpu.SemaphoreType.DMA((ao_size - 1,)),
            pltpu.SemaphoreType.DMA((devices - 1,)),
            pltpu.SemaphoreType.DMA((devices - 1,)),
        ],
        compiler_params=pltpu.CompilerParams(
            collective_id=0, has_side_effects=True, vmem_limit_bytes=60 << 20
        ),
    )(pair, occ_density, virt_density, partner, screen)
    return jnp.sum(terms, axis=0)


def staged_shards(blocks, occ_density, virt_density, partner, screen):
    tile_width = blocks.shape[2]
    aux_count = blocks.shape[4]
    target = partner[0, 0]
    gathered = lax.all_gather(virt_density, "ao", axis=0, tiled=True)
    chosen = lax.dynamic_index_in_dim(gathered, target, 0, keepdims=False)
    pair_block = blocks[0, 0]
    occ_side = jnp.dot(
        occ_density[0],
        pair_block.reshape(tile_width, tile_width * aux_count),
        preferred_element_type=jnp.float32,
    )
    occ_side = occ_side.astype(jnp.bfloat16).reshape(tile_width, tile_width, aux_count)
    dressed = jnp.einsum("mnp,nb->mbp", occ_side, chosen, preferred_element_type=jnp.float32)
    dressed = (dressed * screen[0, 0].astype(jnp.float32)).astype(jnp.bfloat16)
    dressed = dressed.reshape(tile_width * tile_width, aux_count)
    flat_block = pair_block.reshape(tile_width * tile_width, aux_count)
    chi_term = lax.dot_general(
        dressed, flat_block, (((0,), (0,)), ((), ())), preferred_element_type=jnp.float32
    )
    half_sum = lax.psum_scatter(chi_term, "aux", scatter_dimension=0, tiled=True)
    return lax.psum_scatter(half_sum, "ao", scatter_dimension=0, tiled=True)


def solution(mesh):
    aux_size, ao_size = mesh.shape["aux"], mesh.shape["ao"]
    placed = (
        P(("grp", "ao"), "aux", None, None, None),
        P(("grp", "ao"), None, None),
        P(("grp", "ao"), None, None),
        P(("grp", "ao"), "aux"),
        P(("grp", "ao"), "aux"),
    )

    devices = aux_size * ao_size

    def shards(blocks, *rest):
        if blocks.size <= KERNEL_ELEMENTS and devices & (devices - 1) == 0:
            return fused_shards(aux_size, ao_size, blocks, *rest)
        return staged_shards(blocks, *rest)

    return jax.shard_map(
        shards, mesh=mesh, in_specs=placed, out_specs=P(("grp", "aux", "ao"), None), check_vma=False
    )
```

```python
import functools

import jax
import jax.numpy as jnp
from jax import lax
from jax.experimental import pallas as pl
from jax.experimental.pallas import tpu as pltpu
from jax.sharding import PartitionSpec as P

MESH = pl.DeviceIdType.MESH
GROUP = 8
PACK = 4
KERNEL_ELEMENTS = 1 << 18


def flipped(position, mask, count):
    other, bit = position, 1
    while bit < count:
        if mask & bit:
            other = other + (1 - 2 * lax.rem(lax.div(position, bit), 2)) * bit
        bit *= 2
    return other


def packed(rows):
    run = rows.shape[0] // PACK
    return jnp.concatenate([rows[index * run:(index + 1) * run] for index in range(PACK)], axis=1)


def chi_kernel(aux_size, ao_size, blocks_hbm, occ_hbm, virt_hbm, partner_hbm, screen_hbm, incoming,
               pair, occ, own_virt, virts, target, survives, outgoing,
               load_sem, virt_send, virt_recv, chi_send, chi_recv):
    width, aux_count = pair.shape[0], pair.shape[1]
    devices = aux_size * ao_size
    rows = aux_count // devices
    my_aux, my_ao = lax.axis_index("aux"), lax.axis_index("ao")
    me = my_aux * ao_size + my_ao

    peers = []
    for ao_mask in range(ao_size - 1, -1, -1):
        for aux_mask in range(aux_size - 1, -1, -1):
            if ao_mask or aux_mask:
                aux, ao = flipped(my_aux, aux_mask, aux_size), flipped(my_ao, ao_mask, ao_size)
                peers.append((aux * ao_size + ao, {"aux": aux, "ao": ao}))

    barrier = pltpu.get_barrier_semaphore()
    for _, device in peers:
        pl.semaphore_signal(barrier, inc=1, device_id=device, device_id_type=MESH)

    virt_load = pltpu.make_async_copy(virt_hbm.at[0], own_virt, load_sem.at[4])
    virt_load.start()
    loads = [
        pltpu.make_async_copy(blocks_hbm, pair, load_sem.at[0]),
        pltpu.make_async_copy(occ_hbm.at[0], occ, load_sem.at[1]),
        pltpu.make_async_copy(partner_hbm, target, load_sem.at[2]),
        pltpu.make_async_copy(screen_hbm, survives, load_sem.at[3]),
    ]
    for load in loads:
        load.start()
    half = width // 2
    virt_load.wait()
    virts[my_ao] = jnp.concatenate([own_virt[:half], own_virt[half:]], axis=1)

    pl.semaphore_wait(barrier, devices - 1)
    virt_copies = []
    for ao_mask in range(ao_size - 1, 0, -1):
        copy = pltpu.make_async_remote_copy(
            src_ref=virts.at[my_ao], dst_ref=virts.at[my_ao],
            send_sem=virt_send.at[ao_mask - 1], recv_sem=virt_recv.at[ao_mask - 1],
            device_id={"ao": flipped(my_ao, ao_mask, ao_size)}, device_id_type=MESH)
        copy.start()
        virt_copies.append(copy)

    for load in loads:
        load.wait()
    stack = pair[...]
    by_aux = jnp.swapaxes(stack.astype(jnp.float32), 0, 1).astype(jnp.bfloat16)
    occ_block = occ[...]
    left = jnp.stack([
        jnp.dot(occ_block, by_aux[index], preferred_element_type=jnp.float32)
        for index in range(aux_count)
    ])
    left = packed(jnp.swapaxes(left, 0, 1).astype(jnp.bfloat16).reshape(width * aux_count, width))
    flat = packed(stack.reshape(width * aux_count, width))

    for copy in reversed(virt_copies):
        copy.wait_recv()
    chosen = virts[target[0, 0]]
    chosen = jnp.concatenate([chosen[:, :width], chosen[:, width:]], axis=0)
    chosen = jnp.concatenate([chosen] * PACK, axis=1)
    side = lax.div(lax.broadcasted_iota(jnp.int32, chosen.shape, 1), width)
    blank = jnp.zeros_like(chosen)
    diagonal = jnp.concatenate([jnp.where(side == index, chosen, blank) for index in range(PACK)], axis=0)
    right = lax.dot_general(flat, diagonal, (((1,), (1,)), ((), ())), preferred_element_type=jnp.float32)
    right = right.astype(jnp.bfloat16)

    span = GROUP * aux_count
    gram = jnp.zeros((span, span), jnp.float32)
    for start in range(0, flat.shape[0], span):
        gram += lax.dot_general(left[start:start + span], right[start:start + span],
                                (((1,), (1,)), ((), ())), preferred_element_type=jnp.float32)
    lane = lax.broadcasted_iota(jnp.int32, (aux_count, span), 1)
    wide = jnp.zeros((aux_count, span), jnp.float32)
    for index in range(GROUP):
        low = index * aux_count
        wide = jnp.where((lane >= low) & (lane < low + aux_count), gram[low:low + aux_count], wide)
    chi = wide
    while chi.shape[1] > aux_count:
        middle = chi.shape[1] // 2
        chi = chi[:, :middle] + chi[:, middle:]
    chi = chi * survives[0, 0].astype(jnp.float32)

    for index in range(devices):
        outgoing[index] = chi[index * rows:(index + 1) * rows]
    chi_copies = []
    for index, (other, device) in enumerate(peers):
        copy = pltpu.make_async_remote_copy(
            src_ref=outgoing.at[other], dst_ref=incoming.at[me],
            send_sem=chi_send.at[index], recv_sem=chi_recv.at[index],
            device_id=device, device_id_type=MESH)
        copy.start()
        chi_copies.append(copy)
    incoming[me] = outgoing[me]
    for copy in virt_copies + chi_copies:
        copy.wait_send()
    for copy in reversed(chi_copies):
        copy.wait_recv()


def fused_shards(aux_size, ao_size, blocks, occ_density, virt_density, partner, screen):
    width, aux_count = blocks.shape[2], blocks.shape[4]
    devices = aux_size * ao_size
    rows = aux_count // devices
    pair = jnp.swapaxes(blocks[0, 0], 1, 2)
    hbm = pl.BlockSpec(memory_space=pl.ANY)
    terms = pl.pallas_call(
        functools.partial(chi_kernel, aux_size, ao_size),
        out_shape=pltpu.VMEM((devices, rows, aux_count), jnp.float32),
        in_specs=[hbm] * 5,
        out_specs=pl.BlockSpec(memory_space=pltpu.VMEM),
        scratch_shapes=[
            pltpu.VMEM((width, aux_count, width), jnp.bfloat16),
            pltpu.VMEM((width, width), jnp.bfloat16),
            pltpu.VMEM((width, width), jnp.bfloat16),
            pltpu.VMEM((ao_size, width // 2, 2 * width), jnp.bfloat16),
            pltpu.SMEM((1, 1), jnp.int32),
            pltpu.SMEM((1, 1), jnp.int32),
            pltpu.VMEM((devices, rows, aux_count), jnp.float32),
            pltpu.SemaphoreType.DMA((5,)),
            pltpu.SemaphoreType.DMA((ao_size - 1,)),
            pltpu.SemaphoreType.DMA((ao_size - 1,)),
            pltpu.SemaphoreType.DMA((devices - 1,)),
            pltpu.SemaphoreType.DMA((devices - 1,)),
        ],
        compiler_params=pltpu.CompilerParams(
            collective_id=0, has_side_effects=True, vmem_limit_bytes=60 << 20
        ),
    )(pair, occ_density, virt_density, partner, screen)
    return jnp.sum(terms, axis=0)


def staged_shards(blocks, occ_density, virt_density, partner, screen):
    tile_width = blocks.shape[2]
    aux_count = blocks.shape[4]
    target = partner[0, 0]
    gathered = lax.all_gather(virt_density, "ao", axis=0, tiled=True)
    chosen = lax.dynamic_index_in_dim(gathered, target, 0, keepdims=False)
    pair_block = blocks[0, 0]
    occ_side = jnp.dot(
        occ_density[0],
        pair_block.reshape(tile_width, tile_width * aux_count),
        preferred_element_type=jnp.float32,
    )
    occ_side = occ_side.astype(jnp.bfloat16).reshape(tile_width, tile_width, aux_count)
    dressed = jnp.einsum("mnp,nb->mbp", occ_side, chosen, preferred_element_type=jnp.float32)
    dressed = (dressed * screen[0, 0].astype(jnp.float32)).astype(jnp.bfloat16)
    dressed = dressed.reshape(tile_width * tile_width, aux_count)
    flat_block = pair_block.reshape(tile_width * tile_width, aux_count)
    chi_term = lax.dot_general(
        dressed, flat_block, (((0,), (0,)), ((), ())), preferred_element_type=jnp.float32
    )
    half_sum = lax.psum_scatter(chi_term, "aux", scatter_dimension=0, tiled=True)
    return lax.psum_scatter(half_sum, "ao", scatter_dimension=0, tiled=True)


def solution(mesh):
    aux_size, ao_size = mesh.shape["aux"], mesh.shape["ao"]
    placed = (
        P(("grp", "ao"), "aux", None, None, None),
        P(("grp", "ao"), None, None),
        P(("grp", "ao"), None, None),
        P(("grp", "ao"), "aux"),
        P(("grp", "ao"), "aux"),
    )

    devices = aux_size * ao_size

    def shards(blocks, *rest):
        if blocks.size <= KERNEL_ELEMENTS and devices & (devices - 1) == 0:
            return fused_shards(aux_size, ao_size, blocks, *rest)
        return staged_shards(blocks, *rest)

    return jax.shard_map(
        shards, mesh=mesh, in_specs=placed, out_specs=P(("grp", "aux", "ao"), None), check_vma=False
    )
```
